32 devices in a mesh: tm: 4 (over z), owner: 8 (over y, x, core).
Axes of the slice: x: 2, y: 2, z: 4, core: 2. Of those that a mesh axis runs over, the one named last changes fastest.
Arguments:
- pressure: bfloat16 [512, 32768], P('tm', 'owner'), may hold values from -6 to 6
- proj_weight: bfloat16 [8, 32, 4, 128, 128], P('owner', 'tm'), may hold values from -0.25 to 0.25
- pattern: int32 [8, 32, 4], P('owner', 'tm'), may hold values from 0 to 31, as said below
- panel_list: int32 [8, 32], replicated, may hold values from 0 to 191, as said below
- owner_list: int32 [8, 36], replicated, may hold values from -1 to 191, as said below
- owner_count: int32 [8], replicated, may hold values from 12 to 36, as said below
Outputs:
- panel_field: float32 [288, 512, 128], P('owner', 'tm')
The draws below stay inside these ranges and needn't reach their ends.
Inputs may be any that keep to these rules, and one draw needn't show every extreme that they name: `pattern`: the 4 entries of one face block are different. `panel_list`: each row names different panel blocks, owned by 8 different owners, exactly 4 of each. `owner_list`: slots below an owner's count hold its panel blocks; every panel block stands in exactly one such slot; slots from the count on hold -1. `owner_count`: the counts sum to 192.
All inputs are finite; a program needn't handle non-finite values.
Results may differ from the reference program's by a relative error of at most 0.0003.
Values may be sent and summed in bfloat16 or wider, within the bound.
A program may use at most 128 MiB of HBM per device.

```python
import jax
import jax.numpy as jnp
from jax import lax

TIME = 512
BLOCK = 128
KP = 4
FB_DEV = 8
LP = 32
PB_OWN = 24
SLOT = 4
CAP = 36
PANELS = 192
FB_SHARD = 32
FACES = 32768
N_TM = 4
N_OWNER = 8


def ownership(key):
    owner_order = jax.random.permutation(jax.random.fold_in(key, 101), N_OWNER)
    spread = CAP - PB_OWN
    offsets = jax.random.randint(jax.random.fold_in(key, 102), (N_OWNER // 2,), 0, spread + 1)
    offsets = jnp.where(jnp.arange(N_OWNER // 2) == 0, spread, offsets)
    paired = jnp.stack([PB_OWN + offsets, PB_OWN - offsets], axis=1).reshape(-1).astype(jnp.int32)
    counts = jnp.zeros((N_OWNER,), jnp.int32).at[owner_order].set(paired)
    starts = jnp.cumsum(counts) - counts
    shuffled = jax.random.permutation(jax.random.fold_in(key, 103), PB_OWN * N_OWNER).astype(jnp.int32)
    column = jnp.arange(CAP, dtype=jnp.int32)
    position = jnp.minimum(starts[:, None] + column[None, :], PB_OWN * N_OWNER - 1)
    listed = jnp.where(column[None, :] < counts[:, None], shuffled[position], -1)
    return (listed.astype(jnp.int32), counts)


def draw_owner_list(key, part):
    listed, counts = ownership(key)
    return listed


def draw_owner_count(key, part):
    listed, counts = ownership(key)
    return counts


def draw_panel_list(key, part):
    listed, counts = ownership(key)
    groups = LP // SLOT
    rotation = jax.random.randint(jax.random.fold_in(key, 201), (N_OWNER, 1), 0, N_OWNER)
    chosen = (jnp.arange(N_OWNER)[:, None] + rotation + jnp.arange(groups)[None, :]) % N_OWNER
    first_slot = jax.random.randint(jax.random.fold_in(key, 202), (N_OWNER, groups), 0, counts[chosen])
    within = jnp.arange(LP) % SLOT
    member = jnp.arange(LP) // SLOT
    owner_rows = chosen[:, member]
    placing = (first_slot[:, member] + within[None, :]) % counts[owner_rows]
    panels = listed[owner_rows, placing]
    row_keys = jax.random.split(jax.random.fold_in(key, 203), N_OWNER)
    return jax.vmap(jax.random.permutation)(row_keys, panels).astype(jnp.int32)


def draw_pattern(key, part):
    row_count = N_OWNER * N_TM * FB_DEV
    row_keys = jax.random.split(jax.random.fold_in(key, 301), row_count)
    chosen_slots = jax.vmap(lambda row_key: jax.random.permutation(row_key, LP)[:KP])(row_keys)
    return chosen_slots.reshape(N_OWNER, N_TM * FB_DEV, KP).astype(jnp.int32)


def levels(own_key, extent, cuts, smallest, largest):
    loudness, own = 1.0, jax.random.fold_in(own_key, 6)
    for axis_at, parts in cuts:
        heights = jnp.exp(jax.random.uniform(jax.random.fold_in(own, axis_at), (parts,), jnp.float32, smallest / len(cuts), largest / len(cuts)))
        loudness = loudness * jnp.repeat(heights, extent[axis_at] // parts).reshape([-1 if axis == axis_at else 1 for axis in range(len(extent))])
    return loudness


def scatter_about(rng, extent, scale, reach, pieces=(), kind=jnp.bfloat16):
    loudness = levels(rng, extent, pieces, -0.22, 0.18) if pieces else 1.0
    drawn = jax.random.normal(rng, extent, jnp.float32) * scale * loudness
    return jnp.minimum(jnp.maximum(drawn, -reach), reach).astype(kind)


def setup_inputs(seed: int = 0) -> dict:
    seeds = jax.random.split(jax.random.key(seed), 7)
    return {
        "pressure": scatter_about(seeds[0], (TIME, FACES), 1.0, 6.0, ((0, 4), (1, 8))),
        "proj_weight": scatter_about(seeds[1], (N_OWNER, FB_SHARD, KP, BLOCK, BLOCK), (BLOCK * FB_SHARD * KP // LP) ** -0.5, 0.25, ((0, 8), (1, 4))),
        "pattern": draw_pattern(jax.random.fold_in(seeds[6], 71), 0),
        "panel_list": draw_panel_list(jax.random.fold_in(seeds[6], 71), 0),
        "owner_list": draw_owner_list(jax.random.fold_in(seeds[6], 71), 0),
        "owner_count": draw_owner_count(jax.random.fold_in(seeds[6], 71), 0),
    }


def reference(pressure, proj_weight, pattern, panel_list, owner_list, owner_count):
    face_ids = jnp.arange(FB_SHARD, dtype=jnp.int32)

    def shard_step(totals, shard_index):
        weights = proj_weight[shard_index]
        targets = pattern[shard_index]

        def face_step(partial_value, item):
            face_index, weight_rows, target_rows = item
            start = (shard_index * FB_SHARD + face_index) * BLOCK
            face_rows = lax.dynamic_slice_in_dim(pressure, start.astype(jnp.int32), BLOCK, 1)
            contrib = jnp.einsum('ta,kab->ktb', face_rows.astype(jnp.float32), weight_rows.astype(jnp.float32))
            return partial_value.at[target_rows].add(contrib), None

        partial_value, _ = lax.scan(face_step, jnp.zeros((LP, TIME, BLOCK), jnp.float32), (face_ids, weights, targets))
        return totals.at[panel_list[shard_index]].add(partial_value), None

    totals, _ = lax.scan(shard_step, jnp.zeros((PANELS, TIME, BLOCK), jnp.float32), jnp.arange(N_OWNER, dtype=jnp.int32))
    live_slots = jnp.arange(CAP, dtype=jnp.int32)[None, :] < owner_count[:, None]
    picked = totals[jnp.where(live_slots, owner_list, 0)]
    result = jnp.where(live_slots[:, :, None, None], picked, jnp.zeros_like(picked))
    return result.reshape(N_OWNER * CAP, TIME, BLOCK)
```

```python
import functools

import jax
import jax.numpy as jnp
from jax import lax
from jax.experimental import pallas as pl
from jax.experimental.pallas import tpu as pltpu
from jax.sharding import PartitionSpec as P

MESH = pl.DeviceIdType.MESH
PIECES = 4


def gather_kernel(n, w_ref, pat_ref, wg_ref, pg_ref, own_sem, send_sem, recv_sem, psend, precv):
    m = lax.axis_index("tm")
    per = w_ref.shape[0] // PIECES

    barrier = pltpu.get_barrier_semaphore()
    for step in range(1, n):
        pl.semaphore_signal(
            barrier, inc=1, device_id={"tm": lax.rem(m + step, n)}, device_id_type=MESH
        )
    pl.semaphore_wait(barrier, n - 1)

    def part(q):
        return pl.ds(q * per, per)

    own = pltpu.make_async_copy(w_ref, wg_ref.at[m], own_sem.at[0])
    own.start()
    own_pat = pltpu.make_async_copy(pat_ref, pg_ref.at[m], own_sem.at[1])
    own_pat.start()

    def send(way, hop, q):
        toward = m + 1 if way == 0 else m - 1
        origin = m - hop if way == 0 else m + hop
        origin = jnp.clip(origin, 0, n - 1)
        source = w_ref.at[part(q)] if hop == 0 else wg_ref.at[origin, part(q)]
        return pltpu.make_async_remote_copy(
            src_ref=source,
            dst_ref=wg_ref.at[origin, part(q)],
            send_sem=send_sem.at[way, hop, q],
            recv_sem=recv_sem.at[way, hop, q],
            device_id={"tm": jnp.clip(toward, 0, n - 1)},
            device_id_type=MESH,
        )

    def landed(way, hop, q):
        origin = m - 1 - hop if way == 0 else m + 1 + hop
        origin = jnp.clip(origin, 0, n - 1)
        return pltpu.make_async_remote_copy(
            src_ref=w_ref.at[part(q)],
            dst_ref=wg_ref.at[origin, part(q)],
            send_sem=send_sem.at[way, hop, q],
            recv_sem=recv_sem.at[way, hop, q],
            device_id={"tm": lax.rem(m + 1, n)},
            device_id_type=MESH,
        )

    def sends(way, hop):
        return (m - hop >= 0) & (m + 1 < n) if way == 0 else (m + hop < n) & (m >= 1)

    def lands(way, hop):
        return m - 1 - hop >= 0 if way == 0 else m + 1 + hop < n

    for q in range(PIECES):
        for way in range(2):
            @pl.when(sends(way, 0))
            def _():
                send(way, 0, q).start()

    def pat_copy(step):
        return pltpu.make_async_remote_copy(
            src_ref=pat_ref,
            dst_ref=pg_ref.at[m],
            send_sem=psend.at[step],
            recv_sem=precv.at[step],
            device_id={"tm": lax.rem(m + step, n)},
            device_id_type=MESH,
        )

    def pat_landed(step):
        return pltpu.make_async_remote_copy(
            src_ref=pat_ref,
            dst_ref=pg_ref.at[lax.rem(m - step + n, n)],
            send_sem=psend.at[step],
            recv_sem=precv.at[step],
            device_id={"tm": lax.rem(m + step, n)},
            device_id_type=MESH,
        )

    for step in range(1, n):
        pat_copy(step).start()

    for hop in range(n - 1):
        for q in range(PIECES):
            for way in range(2):
                @pl.when(lands(way, hop))
                def _():
                    landed(way, hop, q).wait_recv()
                if hop + 1 < n - 1:
                    @pl.when(sends(way, hop + 1))
                    def _():
                        send(way, hop + 1, q).start()
    for hop in range(n - 1):
        for q in range(PIECES):
            for way in range(2):
                @pl.when(sends(way, hop))
                def _():
                    send(way, hop, q).wait_send()
    for step in range(1, n):
        pat_landed(step).wait_recv()
        pat_copy(step).wait_send()
    own.wait()
    own_pat.wait()


def gather(weights, pattern, n):
    any_space = pl.BlockSpec(memory_space=pl.ANY)
    return pl.pallas_call(
        functools.partial(gather_kernel, n),
        out_shape=(
            jax.ShapeDtypeStruct((n,) + weights.shape, weights.dtype),
            jax.ShapeDtypeStruct((n,) + pattern.shape, pattern.dtype),
        ),
        in_specs=[any_space] * 2,
        out_specs=(any_space, any_space),
        scratch_shapes=[
            pltpu.SemaphoreType.DMA((2,)),
            pltpu.SemaphoreType.DMA((2, n - 1, PIECES)),
            pltpu.SemaphoreType.DMA((2, n - 1, PIECES)),
            pltpu.SemaphoreType.DMA((n,)),
            pltpu.SemaphoreType.DMA((n,)),
        ],
        compiler_params=pltpu.CompilerParams(collective_id=0, has_side_effects=True),
        name="gather_weights",
    )(weights, pattern)


def exchange_kernel(n, in_ref, out_ref, own_sem, send_sem, recv_sem):
    me = lax.axis_index("owner")
    barrier = pltpu.get_barrier_semaphore()
    for step in range(1, n):
        pl.semaphore_signal(
            barrier, inc=1, device_id={"owner": lax.rem(me + step, n)}, device_id_type=MESH
        )
    pl.semaphore_wait(barrier, n - 1)

    def copy(step, landing):
        peer = lax.rem(me + step, n)
        return pltpu.make_async_remote_copy(
            src_ref=in_ref.at[peer],
            dst_ref=out_ref.at[landing],
            send_sem=send_sem.at[step],
            recv_sem=recv_sem.at[step],
            device_id={"owner": peer},
            device_id_type=MESH,
        )

    for step in range(1, n):
        copy(step, me).start()
    own = pltpu.make_async_copy(in_ref.at[me], out_ref.at[me], own_sem)
    own.start()
    for step in range(1, n):
        copy(step, lax.rem(me - step + n, n)).wait_recv()
        copy(step, me).wait_send()
    own.wait()


def exchange(packed, n):
    any_space = pl.BlockSpec(memory_space=pl.ANY)
    return pl.pallas_call(
        functools.partial(exchange_kernel, n),
        out_shape=jax.ShapeDtypeStruct(packed.shape, packed.dtype),
        in_specs=[any_space],
        out_specs=any_space,
        scratch_shapes=[
            pltpu.SemaphoreType.DMA,
            pltpu.SemaphoreType.DMA((n,)),
            pltpu.SemaphoreType.DMA((n,)),
        ],
        compiler_params=pltpu.CompilerParams(collective_id=1, has_side_effects=True),
        name="exchange_sums",
    )(packed)


def product_kernel(fb, kp, rows_ref, p_ref, w_ref, out_ref):
    g = pl.program_id(0)

    @pl.when(g == 0)
    def _():
        out_ref[...] = jnp.zeros_like(out_ref)

    block = w_ref.shape[-1]
    for i in range(fb):
        x = p_ref[:, i * block : (i + 1) * block]
        for k in range(kp):
            row = rows_ref[(g * fb + i) * kp + k]
            out_ref[row] += jnp.dot(x, w_ref[0, i, k], preferred_element_type=jnp.float32)


def products(rows, pressure, gathered, list_len):
    n, fb, kp, block, _ = gathered.shape
    time_len = pressure.shape[0]
    return pl.pallas_call(
        functools.partial(product_kernel, fb, kp),
        out_shape=jax.ShapeDtypeStruct((list_len, time_len, block), jnp.float32),
        grid_spec=pltpu.PrefetchScalarGridSpec(
            num_scalar_prefetch=1,
            grid=(n,),
            in_specs=[
                pl.BlockSpec((time_len, fb * block), lambda g, rows: (0, g)),
                pl.BlockSpec((1, fb, kp, block, block), lambda g, rows: (g, 0, 0, 0, 0)),
            ],
            out_specs=pl.BlockSpec(
                (list_len, time_len, block), lambda g, rows: (0, 0, 0)
            ),
        ),
        compiler_params=pltpu.CompilerParams(vmem_limit_bytes=32 * 1024 * 1024),
        name="products",
    )(rows, pressure, gathered)


def collect_kernel(count, dest_ref, in_ref, out_ref):
    out_ref[...] = jnp.zeros_like(out_ref)

    def step(e, carry):
        out_ref[dest_ref[e]] += in_ref[e].astype(jnp.float32)
        return carry

    lax.fori_loop(0, count, step, 0)


def collect(dest, received, capacity):
    count, time_len, block = received.shape
    return pl.pallas_call(
        functools.partial(collect_kernel, count),
        out_shape=jax.ShapeDtypeStruct((capacity, time_len, block), jnp.float32),
        grid_spec=pltpu.PrefetchScalarGridSpec(
            num_scalar_prefetch=1,
            grid=(1,),
            in_specs=[pl.BlockSpec(received.shape, lambda g, dest: (0, 0, 0))],
            out_specs=pl.BlockSpec(
                (capacity, time_len, block), lambda g, dest: (0, 0, 0)
            ),
        ),
        compiler_params=pltpu.CompilerParams(vmem_limit_bytes=32 * 1024 * 1024),
        name="collect",
    )(dest, received)


def tables(panel_list, owner_list, owner_count, own, slots):
    owners, list_len = panel_list.shape
    capacity = owner_list.shape[1]
    live = jnp.arange(capacity, dtype=jnp.int32)[None, :] < owner_count[:, None]
    listed = jnp.where(live, owner_list, -1).reshape(1, -1)
    place = jnp.arange(owners * capacity, dtype=jnp.int32)[None, :]
    found = jnp.sum(
        jnp.where(panel_list.reshape(-1, 1) == listed, place, 0), axis=1, dtype=jnp.int32
    ).reshape(owners, list_len)
    target, slot = found // capacity, found % capacity
    position = jnp.arange(list_len, dtype=jnp.int32)
    earlier = (target[:, None, :] == target[:, :, None]) & (
        position[None, None, :] < position[None, :, None]
    )
    rank = jnp.sum(earlier, axis=2, dtype=jnp.int32)
    packed_row = target * slots + rank
    wanted = own * slots + jnp.arange(slots, dtype=jnp.int32)
    dest = jnp.sum(
        jnp.where(packed_row[:, None, :] == wanted[None, :, None], slot[:, None, :], 0),
        axis=2,
        dtype=jnp.int32,
    )
    return packed_row[own], dest.reshape(-1)


def body(n_tm, n_owner, pressure, proj_weight, pattern, panel_list, owner_list, owner_count):
    own = lax.axis_index("owner")
    list_len = panel_list.shape[1]
    capacity = owner_list.shape[1]
    slots = list_len // n_owner
    packed_row, dest = tables(panel_list, owner_list, owner_count, own, slots)
    fb, kp = pattern.shape[1:]
    rows = packed_row[pattern[0].reshape(-1)].reshape(1, -1)
    rows = jnp.pad(rows, ((0, 7), (0, 128 - rows.shape[1])))
    gathered, rows = gather(proj_weight[0], rows, n_tm)
    rows = rows[:, 0, : fb * kp].reshape(-1)
    packed = products(rows, pressure, gathered, list_len)
    block_shape = packed.shape[1:]
    received = exchange(packed.reshape((n_owner, slots) + block_shape), n_owner)
    return collect(dest, received.reshape((list_len,) + block_shape), capacity)


def solution(mesh):
    placed = (
        P("tm", "owner"),
        P("owner", "tm", None, None, None),
        P("owner", "tm", None),
        P(),
        P(),
        P(),
    )
    return jax.shard_map(
        functools.partial(body, mesh.shape["tm"], mesh.shape["owner"]),
        mesh=mesh,
        in_specs=placed,
        out_specs=P("owner", "tm", None),
        check_vma=False,
    )
```

```python
import functools

import jax
import jax.numpy as jnp
from jax import lax
from jax.experimental import pallas as pl
from jax.experimental.pallas import tpu as pltpu
from jax.sharding import PartitionSpec as P

MESH = pl.DeviceIdType.MESH
PIECES = 4


def turn_kernel(n, w_ref, pat_ref, wt_ref, pg_ref, send_sem, recv_sem):
    m = lax.axis_index("tm")
    barrier = pltpu.get_barrier_semaphore()
    for step in range(1, n):
        pl.semaphore_signal(
            barrier, inc=1, device_id={"tm": lax.rem(m + step, n)}, device_id_type=MESH
        )
    pl.semaphore_wait(barrier, n - 1)

    def copy(step, landing):
        return pltpu.make_async_remote_copy(
            src_ref=pat_ref,
            dst_ref=pg_ref.at[landing],
            send_sem=send_sem.at[step],
            recv_sem=recv_sem.at[step],
            device_id={"tm": lax.rem(m + step, n)},
            device_id_type=MESH,
        )

    for step in range(1, n):
        copy(step, m).start()
    pg_ref[m] = pat_ref[...]
    rows = w_ref.shape[-1] // PIECES
    kp = w_ref.shape[1]

    def turn(i, carry):
        for k in range(kp):
            t = w_ref[i, k].T
            for c in range(PIECES):
                wt_ref[c, i, k] = t[c * rows : (c + 1) * rows]
        return carry

    lax.fori_loop(0, w_ref.shape[0], turn, 0)
    for step in range(1, n):
        copy(step, lax.rem(m - step + n, n)).wait_recv()
        copy(step, m).wait_send()


def turn(weights, pattern, n):
    fb, kp, faces, panels = weights.shape
    vmem = pl.BlockSpec(memory_space=pltpu.VMEM)
    return pl.pallas_call(
        functools.partial(turn_kernel, n),
        out_shape=(
            jax.ShapeDtypeStruct((PIECES, fb, kp, panels // PIECES, faces), weights.dtype),
            jax.ShapeDtypeStruct((n,) + pattern.shape, pattern.dtype),
        ),
        in_specs=[vmem] * 2,
        out_specs=(vmem, vmem),
        scratch_shapes=[
            pltpu.SemaphoreType.DMA((n,)),
            pltpu.SemaphoreType.DMA((n,)),
        ],
        compiler_params=pltpu.CompilerParams(
            collective_id=0, has_side_effects=True, vmem_limit_bytes=32 * 1024 * 1024
        ),
        name="turn_weights",
    )(weights, pattern)


def fused_kernel(
    n, owners, hit_ref, last_ref, w_ref, p_ref, out_ref,
    wg, terms, runs, outgoing, wsend, wrecv, osend, orecv, own_sem,
):
    m = lax.axis_index("tm")
    me = lax.axis_index("owner")
    pieces, fb, kp, rows, block = w_ref.shape
    time_len = p_ref.shape[0]
    hits = terms.shape[0]
    slots = out_ref.shape[1]

    barrier = pltpu.get_barrier_semaphore()
    for step in range(1, n):
        pl.semaphore_signal(
            barrier, inc=1, device_id={"tm": lax.rem(m + step, n)}, device_id_type=MESH
        )
    for step in range(1, owners):
        pl.semaphore_signal(
            barrier, inc=1, device_id={"owner": lax.rem(me + step, owners)}, device_id_type=MESH
        )
    pl.semaphore_wait(barrier, n + owners - 2)

    def origin_of(way, hop):
        return jnp.clip(m - hop if way == 0 else m + hop, 0, n - 1)

    def send(way, hop, c):
        origin = origin_of(way, hop)
        toward = m + 1 if way == 0 else m - 1
        return pltpu.make_async_remote_copy(
            src_ref=w_ref.at[c] if hop == 0 else wg.at[c, origin],
            dst_ref=wg.at[c, origin],
            send_sem=wsend.at[way, hop, c],
            recv_sem=wrecv.at[way, hop, c],
            device_id={"tm": jnp.clip(toward, 0, n - 1)},
            device_id_type=MESH,
        )

    def landed(way, hop, c):
        return pltpu.make_async_remote_copy(
            src_ref=w_ref.at[c],
            dst_ref=wg.at[c, origin_of(way, hop + 1)],
            send_sem=wsend.at[way, hop, c],
            recv_sem=wrecv.at[way, hop, c],
            device_id={"tm": lax.rem(m + 1, n)},
            device_id_type=MESH,
        )

    def sends(way, hop):
        return (m - hop >= 0) & (m + 1 < n) if way == 0 else (m + hop < n) & (m >= 1)

    def lands(way, hop):
        return m - 1 - hop >= 0 if way == 0 else m + 1 + hop < n

    def start_own(c):
        for way in range(2):
            @pl.when(sends(way, 0))
            def _():
                send(way, 0, c).start()

    def product(weights, origin):
        for i in range(fb):
            face = origin * fb + i
            x = p_ref[:, pl.ds(pl.multiple_of(face * block, block), block)]
            y = lax.dot_general(
                weights(i).reshape(kp * rows, block), x, (((1,), (1,)), ((), ())),
                preferred_element_type=jnp.float32,
            )
            terms[pl.ds(face * kp, kp)] = y.reshape(kp, rows, time_len)

    def give(c, step, landing):
        peer = lax.rem(me + step, owners)
        return pltpu.make_async_remote_copy(
            src_ref=outgoing.at[c, peer],
            dst_ref=out_ref.at[landing, :, c],
            send_sem=osend.at[c, step],
            recv_sem=orecv.at[c, step],
            device_id={"owner": peer},
            device_id_type=MESH,
        )

    def keep(c):
        return pltpu.make_async_copy(outgoing.at[c, me], out_ref.at[me, :, c], own_sem.at[c])

    for c in range(min(2, pieces)):
        start_own(c)

    def piece(c, carry):
        product(lambda i: w_ref[c, i], m)
        for hop in range(n - 1):
            for way in range(2):
                @pl.when(lands(way, hop))
                def _():
                    landed(way, hop, c).wait_recv()
                if hop + 1 < n - 1:
                    @pl.when(sends(way, hop + 1))
                    def _():
                        send(way, hop + 1, c).start()
            if hop == 0:
                @pl.when(c + 2 < pieces)
                def _():
                    start_own(c + 2)
            for way in range(2):
                @pl.when(lands(way, hop))
                def _():
                    origin = origin_of(way, hop + 1)
                    product(lambda i: wg[c, origin, i], origin)

        def run(h, total):
            code = hit_ref[h]
            term = terms[code >> 1]
            total = jnp.where((code & 1) == 1, term, total + term)
            runs[h] = total
            return total

        lax.fori_loop(0, hits, run, jnp.zeros((rows, time_len), jnp.float32), unroll=8)
        for peer in range(owners):
            for slot in range(slots):
                code = last_ref[peer * slots + slot]
                total = runs[code >> 1]
                outgoing[c, peer, slot] = jnp.where((code & 1) == 1, total, jnp.zeros_like(total))
        for step in range(1, owners):
            give(c, step, me).start()
        keep(c).start()
        return carry

    lax.fori_loop(0, pieces, piece, 0)

    def finish(c, carry):
        for hop in range(n - 1):
            for way in range(2):
                @pl.when(sends(way, hop))
                def _():
                    send(way, hop, c).wait_send()
        for step in range(1, owners):
            give(c, step, lax.rem(me - step + owners, owners)).wait_recv()
            give(c, step, me).wait_send()
        keep(c).wait()
        return carry

    lax.fori_loop(0, pieces, finish, 0)


def fused(hit, last, turned, pressure, n, owners):
    pieces, fb, kp, rows, block = turned.shape
    time_len = pressure.shape[0]
    slots = last.shape[0] // owners
    hits = hit.shape[0]
    smem = pl.BlockSpec(memory_space=pltpu.SMEM)
    vmem = pl.BlockSpec(memory_space=pltpu.VMEM)
    return pl.pallas_call(
        functools.partial(fused_kernel, n, owners),
        out_shape=jax.ShapeDtypeStruct((owners, slots, pieces, rows, time_len), jnp.float32),
        in_specs=[smem, smem, vmem, vmem],
        out_specs=pl.BlockSpec(memory_space=pl.ANY),
        scratch_shapes=[
            pltpu.VMEM((pieces, n, fb, kp, rows, block), turned.dtype),
            pltpu.VMEM((hits, rows, time_len), jnp.float32),
            pltpu.VMEM((hits, rows, time_len), jnp.float32),
            pltpu.VMEM((pieces, owners, slots, rows, time_len), jnp.float32),
            pltpu.SemaphoreType.DMA((2, n - 1, pieces)),
            pltpu.SemaphoreType.DMA((2, n - 1, pieces)),
            pltpu.SemaphoreType.DMA((pieces, owners)),
            pltpu.SemaphoreType.DMA((pieces, owners)),
            pltpu.SemaphoreType.DMA((pieces,)),
        ],
        compiler_params=pltpu.CompilerParams(
            collective_id=1, has_side_effects=True, vmem_limit_bytes=48 * 1024 * 1024
        ),
        name="gather_multiply_exchange",
    )(hit, last, turned, pressure)


def hit_tables(rows, count):
    order = jnp.arange(rows.shape[0], dtype=jnp.int32)
    same = rows[:, None] == rows[None, :]
    before = order[None, :] < order[:, None]
    ahead = (rows[None, :] < rows[:, None]) | (same & before)
    rank = jnp.sum(ahead, axis=1, dtype=jnp.int32)
    first = 1 - jnp.any(same & before, axis=1).astype(jnp.int32)
    code = 2 * order + first
    hit = jnp.sum(
        jnp.where(rank[:, None] == order[None, :], code[:, None], 0), axis=0, dtype=jnp.int32
    )
    wanted = jnp.arange(count, dtype=jnp.int32)
    upto = jnp.sum(rows[None, :] <= wanted[:, None], axis=1, dtype=jnp.int32)
    there = jnp.any(rows[None, :] == wanted[:, None], axis=1).astype(jnp.int32)
    return hit, 2 * jnp.maximum(upto - 1, 0) + there


def collect_kernel(count, dest_ref, in_ref, out_ref):
    out_ref[...] = jnp.zeros_like(out_ref)

    def step(e, carry):
        out_ref[dest_ref[e]] += in_ref[e].T
        return carry

    lax.fori_loop(0, count, step, 0)


def collect(dest, received, capacity):
    count, block, time_len = received.shape
    return pl.pallas_call(
        functools.partial(collect_kernel, count),
        out_shape=jax.ShapeDtypeStruct((capacity, time_len, block), jnp.float32),
        grid_spec=pltpu.PrefetchScalarGridSpec(
            num_scalar_prefetch=1,
            grid=(1,),
            in_specs=[pl.BlockSpec(received.shape, lambda g, dest: (0, 0, 0))],
            out_specs=pl.BlockSpec(
                (capacity, time_len, block), lambda g, dest: (0, 0, 0)
            ),
        ),
        compiler_params=pltpu.CompilerParams(vmem_limit_bytes=32 * 1024 * 1024),
        name="collect",
    )(dest, received)


def tables(panel_list, owner_list, owner_count, own, slots):
    owners, list_len = panel_list.shape
    capacity = owner_list.shape[1]
    live = jnp.arange(capacity, dtype=jnp.int32)[None, :] < owner_count[:, None]
    listed = jnp.where(live, owner_list, -1).reshape(1, -1)
    place = jnp.arange(owners * capacity, dtype=jnp.int32)[None, :]
    found = jnp.sum(
        jnp.where(panel_list.reshape(-1, 1) == listed, place, 0), axis=1, dtype=jnp.int32
    ).reshape(owners, list_len)
    target, slot = found // capacity, found % capacity
    position = jnp.arange(list_len, dtype=jnp.int32)
    earlier = (target[:, None, :] == target[:, :, None]) & (
        position[None, None, :] < position[None, :, None]
    )
    rank = jnp.sum(earlier, axis=2, dtype=jnp.int32)
    packed_row = target * slots + rank
    wanted = own * slots + jnp.arange(slots, dtype=jnp.int32)
    dest = jnp.sum(
        jnp.where(packed_row[:, None, :] == wanted[None, :, None], slot[:, None, :], 0),
        axis=2,
        dtype=jnp.int32,
    )
    return packed_row[own], dest.reshape(-1)


def body(n_tm, n_owner, pressure, proj_weight, pattern, panel_list, owner_list, owner_count):
    own = lax.axis_index("owner")
    list_len = panel_list.shape[1]
    capacity = owner_list.shape[1]
    slots = list_len // n_owner
    packed_row, dest = tables(panel_list, owner_list, owner_count, own, slots)
    fb, kp = pattern.shape[1:]
    rows = packed_row[pattern[0].reshape(-1)].reshape(1, -1)
    rows = jnp.pad(rows, ((0, 7), (0, 128 - rows.shape[1])))
    turned, rows = turn(proj_weight[0], rows, n_tm)
    rows = rows[:, 0, : fb * kp].reshape(-1)
    hit, last = hit_tables(rows, list_len)
    received = fused(hit, last, turned, pressure, n_tm, n_owner)
    time_len = pressure.shape[0]
    return collect(dest, received.reshape(list_len, -1, time_len), capacity)


def solution(mesh):
    placed = (
        P("tm", "owner"),
        P("owner", "tm", None, None, None),
        P("owner", "tm", None),
        P(),
        P(),
        P(),
    )
    return jax.shard_map(
        functools.partial(body, mesh.shape["tm"], mesh.shape["owner"]),
        mesh=mesh,
        in_specs=placed,
        out_specs=P("owner", "tm", None),
        check_vma=False,
    )
```

```python
import functools

import jax
import jax.numpy as jnp
from jax import lax
from jax.experimental import pallas as pl
from jax.experimental.pallas import tpu as pltpu
from jax.sharding import PartitionSpec as P

MESH = pl.DeviceIdType.MESH
PIECES = 4
LOCAL = 2


def turn_kernel(n, w_ref, pat_ref, wt_ref, pg_ref, send_sem, recv_sem):
    m = lax.axis_index("tm")
    barrier = pltpu.get_barrier_semaphore()
    for step in range(1, n):
        pl.semaphore_signal(
            barrier, inc=1, device_id={"tm": lax.rem(m + step, n)}, device_id_type=MESH
        )
    pl.semaphore_wait(barrier, n - 1)

    def copy(step, landing):
        return pltpu.make_async_remote_copy(
            src_ref=pat_ref,
            dst_ref=pg_ref.at[landing],
            send_sem=send_sem.at[step],
            recv_sem=recv_sem.at[step],
            device_id={"tm": lax.rem(m + step, n)},
            device_id_type=MESH,
        )

    for step in range(1, n):
        copy(step, m).start()
    pg_ref[m] = pat_ref[...]
    rows = w_ref.shape[-1] // PIECES
    kp = w_ref.shape[1]

    def turn(i, carry):
        for k in range(kp):
            t = w_ref[i, k].T
            for c in range(PIECES):
                wt_ref[c, i, k] = t[c * rows : (c + 1) * rows]
        return carry

    lax.fori_loop(0, w_ref.shape[0], turn, 0)
    for step in range(1, n):
        copy(step, lax.rem(m - step + n, n)).wait_recv()
        copy(step, m).wait_send()


def turn(weights, pattern, n):
    fb, kp, faces, panels = weights.shape
    vmem = pl.BlockSpec(memory_space=pltpu.VMEM)
    return pl.pallas_call(
        functools.partial(turn_kernel, n),
        out_shape=(
            jax.ShapeDtypeStruct((PIECES, fb, kp, panels // PIECES, faces), weights.dtype),
            jax.ShapeDtypeStruct((n,) + pattern.shape, pattern.dtype),
        ),
        in_specs=[vmem] * 2,
        out_specs=(vmem, vmem),
        scratch_shapes=[
            pltpu.SemaphoreType.DMA((n,)),
            pltpu.SemaphoreType.DMA((n,)),
        ],
        compiler_params=pltpu.CompilerParams(
            collective_id=0, has_side_effects=True, vmem_limit_bytes=32 * 1024 * 1024
        ),
        name="turn_weights",
    )(weights, pattern)


def fused_kernel(
    n, owners, hit_ref, last_ref, w_ref, p_ref, out_ref,
    wg, terms, runs, outgoing, lent, outgoing2, wsend, wrecv, osend, orecv, own_sem, lent_sem, osend2,
):
    m = lax.axis_index("tm")
    me = lax.axis_index("owner")
    pieces, fb, kp, rows, block = w_ref.shape
    time_len = p_ref.shape[0]
    hits = terms.shape[0]
    slots = out_ref.shape[1]

    barrier = pltpu.get_barrier_semaphore()
    for step in range(1, n):
        pl.semaphore_signal(
            barrier, inc=1, device_id={"tm": lax.rem(m + step, n)}, device_id_type=MESH
        )
    for step in range(1, owners):
        pl.semaphore_signal(
            barrier, inc=1, device_id={"owner": lax.rem(me + step, owners)}, device_id_type=MESH
        )
    is_end = (m == 0) | (m == n - 1)
    helps = (m == 1) | (m == n - 2)
    near = jnp.where(m < n // 2, 1, n - 2)
    far = jnp.where(m < n // 2, 0, n - 1)

    @pl.when(is_end)
    def _():
        for step in range(owners):
            pl.semaphore_signal(
                barrier, inc=1, device_id={"tm": near, "owner": lax.rem(me + step, owners)},
                device_id_type=MESH,
            )

    pl.semaphore_wait(barrier, n + owners - 2 + jnp.where(helps, owners, 0))

    def lend():
        return pltpu.make_async_remote_copy(
            src_ref=p_ref,
            dst_ref=lent,
            send_sem=lent_sem.at[0],
            recv_sem=lent_sem.at[1],
            device_id={"tm": near},
            device_id_type=MESH,
        )

    def origin_of(way, hop):
        return jnp.clip(m - hop if way == 0 else m + hop, 0, n - 1)

    def send(way, hop, c):
        origin = origin_of(way, hop)
        toward = m + 1 if way == 0 else m - 1
        return pltpu.make_async_remote_copy(
            src_ref=w_ref.at[c] if hop == 0 else wg.at[c, origin],
            dst_ref=wg.at[c, origin],
            send_sem=wsend.at[way, hop, c],
            recv_sem=wrecv.at[way, hop, c],
            device_id={"tm": jnp.clip(toward, 0, n - 1)},
            device_id_type=MESH,
        )

    def landed(way, hop, c):
        return pltpu.make_async_remote_copy(
            src_ref=w_ref.at[c],
            dst_ref=wg.at[c, origin_of(way, hop + 1)],
            send_sem=wsend.at[way, hop, c],
            recv_sem=wrecv.at[way, hop, c],
            device_id={"tm": lax.rem(m + 1, n)},
            device_id_type=MESH,
        )

    def edge(c):
        return jnp.where(c >= LOCAL, 1, 0)

    def sends(way, hop, c):
        if way == 0:
            return (m - hop >= 0) & (m + 1 < n - edge(c))
        return (m + hop < n) & (m - 1 >= edge(c))

    def lands(way, hop, c):
        if way == 0:
            return (m - 1 - hop >= 0) & (m < n - edge(c))
        return (m + 1 + hop < n) & (m >= edge(c))

    def start_own(c):
        for way in range(2):
            @pl.when(sends(way, 0, c))
            def _():
                send(way, 0, c).start()

    def product(weights, origin, p_ref):
        for i in range(fb):
            face = origin * fb + i
            x = p_ref[:, pl.ds(pl.multiple_of(face * block, block), block)]
            y = lax.dot_general(
                weights(i).reshape(kp * rows, block), x, (((1,), (1,)), ((), ())),
                preferred_element_type=jnp.float32,
            )
            terms[pl.ds(face * kp, kp)] = y.reshape(kp, rows, time_len)

    def give(c, step, landing):
        peer = lax.rem(me + step, owners)
        return pltpu.make_async_remote_copy(
            src_ref=outgoing.at[c, peer],
            dst_ref=out_ref.at[landing, :, c],
            send_sem=osend.at[c, step],
            recv_sem=orecv.at[c, step],
            device_id={"owner": peer},
            device_id_type=MESH,
        )

    def keep(c):
        return pltpu.make_async_copy(outgoing.at[c, me], out_ref.at[me, :, c], own_sem.at[c])

    def give2(c, step, landing):
        peer = lax.rem(me + step, owners)
        return pltpu.make_async_remote_copy(
            src_ref=outgoing2.at[jnp.maximum(c - LOCAL, 0), peer],
            dst_ref=out_ref.at[landing, :, c],
            send_sem=osend2.at[c, step],
            recv_sem=orecv.at[c, step],
            device_id={"tm": far, "owner": peer},
            device_id_type=MESH,
        )

    def run(h, total):
        code = hit_ref[h]
        term = terms[code >> 1]
        total = jnp.where((code & 1) == 1, term, total + term)
        runs[h] = total
        return total

    def sum_up(target, at):
        lax.fori_loop(0, hits, run, jnp.zeros((rows, time_len), jnp.float32), unroll=8)
        for peer in range(owners):
            for slot in range(slots):
                code = last_ref[peer * slots + slot]
                total = runs[code >> 1]
                target[at, peer, slot] = jnp.where((code & 1) == 1, total, jnp.zeros_like(total))

    for c in range(LOCAL):
        start_own(c)

    @pl.when(is_end)
    def _():
        lend().start()

    def piece(c, carry):
        at_home = jnp.logical_not(is_end) | (c < LOCAL)

        @pl.when(at_home)
        def _():
            product(lambda i: w_ref[c, i], m, p_ref)

        for hop in range(n - 1):
            for way in range(2):
                @pl.when(lands(way, hop, c))
                def _():
                    landed(way, hop, c).wait_recv()
                if hop + 1 < n - 1:
                    @pl.when(sends(way, hop + 1, c))
                    def _():
                        send(way, hop + 1, c).start()
            if hop == 0:
                @pl.when(c + LOCAL < pieces)
                def _():
                    start_own(c + LOCAL)
            for way in range(2):
                @pl.when(lands(way, hop, c))
                def _():
                    origin = origin_of(way, hop + 1)
                    product(lambda i: wg[c, origin, i], origin, p_ref)

        @pl.when(at_home)
        def _():
            sum_up(outgoing, c)
            for step in range(1, owners):
                give(c, step, me).start()
            keep(c).start()

        @pl.when(helps & (c == LOCAL))
        def _():
            lend().wait_recv()

        @pl.when(helps & (c >= LOCAL))
        def _():
            product(lambda i: w_ref[c, i], m, lent)

            def other(step, carry):
                origin = lax.rem(m + step, n)
                product(lambda i: wg[c, origin, i], origin, lent)
                return carry

            lax.fori_loop(1, n, other, 0)
            sum_up(outgoing2, c - LOCAL)
            for step in range(owners):
                give2(c, step, me).start()

        return carry

    lax.fori_loop(0, pieces, piece, 0)

    def finish(c, carry):
        at_home = jnp.logical_not(is_end) | (c < LOCAL)
        for hop in range(n - 1):
            for way in range(2):
                @pl.when(sends(way, hop, c))
                def _():
                    send(way, hop, c).wait_send()
        for step in range(1, owners):
            give(c, step, lax.rem(me - step + owners, owners)).wait_recv()

        @pl.when(at_home)
        def _():
            for step in range(1, owners):
                give(c, step, me).wait_send()
            keep(c).wait()

        @pl.when(jnp.logical_not(at_home))
        def _():
            give2(c, 0, me).wait_recv()

        @pl.when(helps & (c >= LOCAL))
        def _():
            for step in range(owners):
                give2(c, step, me).wait_send()

        return carry

    lax.fori_loop(0, pieces, finish, 0)

    @pl.when(is_end)
    def _():
        lend().wait_send()


def fused(hit, last, turned, pressure, n, owners):
    pieces, fb, kp, rows, block = turned.shape
    time_len = pressure.shape[0]
    slots = last.shape[0] // owners
    hits = hit.shape[0]
    smem = pl.BlockSpec(memory_space=pltpu.SMEM)
    vmem = pl.BlockSpec(memory_space=pltpu.VMEM)
    return pl.pallas_call(
        functools.partial(fused_kernel, n, owners),
        out_shape=jax.ShapeDtypeStruct((owners, slots, pieces, rows, time_len), jnp.float32),
        in_specs=[smem, smem, vmem, vmem],
        out_specs=pl.BlockSpec(memory_space=pl.ANY),
        scratch_shapes=[
            pltpu.VMEM((pieces, n, fb, kp, rows, block), turned.dtype),
            pltpu.VMEM((hits, rows, time_len), jnp.float32),
            pltpu.VMEM((hits, rows, time_len), jnp.float32),
            pltpu.VMEM((pieces, owners, slots, rows, time_len), jnp.float32),
            pltpu.VMEM(pressure.shape, pressure.dtype),
            pltpu.VMEM((pieces - LOCAL, owners, slots, rows, time_len), jnp.float32),
            pltpu.SemaphoreType.DMA((2, n - 1, pieces)),
            pltpu.SemaphoreType.DMA((2, n - 1, pieces)),
            pltpu.SemaphoreType.DMA((pieces, owners)),
            pltpu.SemaphoreType.DMA((pieces, owners)),
            pltpu.SemaphoreType.DMA((pieces,)),
            pltpu.SemaphoreType.DMA((2,)),
            pltpu.SemaphoreType.DMA((pieces, owners)),
        ],
        compiler_params=pltpu.CompilerParams(
            collective_id=1, has_side_effects=True, vmem_limit_bytes=48 * 1024 * 1024
        ),
        name="gather_multiply_exchange",
    )(hit, last, turned, pressure)


def hit_tables(rows, count):
    order = jnp.arange(rows.shape[0], dtype=jnp.int32)
    same = rows[:, None] == rows[None, :]
    before = order[None, :] < order[:, None]
    ahead = (rows[None, :] < rows[:, None]) | (same & before)
    rank = jnp.sum(ahead, axis=1, dtype=jnp.int32)
    first = 1 - jnp.any(same & before, axis=1).astype(jnp.int32)
    code = 2 * order + first
    hit = jnp.sum(
        jnp.where(rank[:, None] == order[None, :], code[:, None], 0), axis=0, dtype=jnp.int32
    )
    wanted = jnp.arange(count, dtype=jnp.int32)
    upto = jnp.sum(rows[None, :] <= wanted[:, None], axis=1, dtype=jnp.int32)
    there = jnp.any(rows[None, :] == wanted[:, None], axis=1).astype(jnp.int32)
    return hit, 2 * jnp.maximum(upto - 1, 0) + there


def collect_kernel(count, dest_ref, in_ref, out_ref):
    out_ref[...] = jnp.zeros_like(out_ref)

    def step(e, carry):
        out_ref[dest_ref[e]] += in_ref[e].T
        return carry

    lax.fori_loop(0, count, step, 0)


def collect(dest, received, capacity):
    count, block, time_len = received.shape
    return pl.pallas_call(
        functools.partial(collect_kernel, count),
        out_shape=jax.ShapeDtypeStruct((capacity, time_len, block), jnp.float32),
        grid_spec=pltpu.PrefetchScalarGridSpec(
            num_scalar_prefetch=1,
            grid=(1,),
            in_specs=[pl.BlockSpec(received.shape, lambda g, dest: (0, 0, 0))],
            out_specs=pl.BlockSpec(
                (capacity, time_len, block), lambda g, dest: (0, 0, 0)
            ),
        ),
        compiler_params=pltpu.CompilerParams(vmem_limit_bytes=32 * 1024 * 1024),
        name="collect",
    )(dest, received)


def tables(panel_list, owner_list, owner_count, own, slots):
    owners, list_len = panel_list.shape
    capacity = owner_list.shape[1]
    live = jnp.arange(capacity, dtype=jnp.int32)[None, :] < owner_count[:, None]
    listed = jnp.where(live, owner_list, -1).reshape(1, -1)
    place = jnp.arange(owners * capacity, dtype=jnp.int32)[None, :]
    found = jnp.sum(
        jnp.where(panel_list.reshape(-1, 1) == listed, place, 0), axis=1, dtype=jnp.int32
    ).reshape(owners, list_len)
    target, slot = found // capacity, found % capacity
    position = jnp.arange(list_len, dtype=jnp.int32)
    earlier = (target[:, None, :] == target[:, :, None]) & (
        position[None, None, :] < position[None, :, None]
    )
    rank = jnp.sum(earlier, axis=2, dtype=jnp.int32)
    packed_row = target * slots + rank
    wanted = own * slots + jnp.arange(slots, dtype=jnp.int32)
    dest = jnp.sum(
        jnp.where(packed_row[:, None, :] == wanted[None, :, None], slot[:, None, :], 0),
        axis=2,
        dtype=jnp.int32,
    )
    return packed_row[own], dest.reshape(-1)


def body(n_tm, n_owner, pressure, proj_weight, pattern, panel_list, owner_list, owner_count):
    own = lax.axis_index("owner")
    list_len = panel_list.shape[1]
    capacity = owner_list.shape[1]
    slots = list_len // n_owner
    packed_row, dest = tables(panel_list, owner_list, owner_count, own, slots)
    fb, kp = pattern.shape[1:]
    rows = packed_row[pattern[0].reshape(-1)].reshape(1, -1)
    rows = jnp.pad(rows, ((0, 7), (0, 128 - rows.shape[1])))
    turned, rows = turn(proj_weight[0], rows, n_tm)
    rows = rows[:, 0, : fb * kp].reshape(-1)
    hit, last = hit_tables(rows, list_len)
    received = fused(hit, last, turned, pressure, n_tm, n_owner)
    time_len = pressure.shape[0]
    return collect(dest, received.reshape(list_len, -1, time_len), capacity)


def solution(mesh):
    placed = (
        P("tm", "owner"),
        P("owner", "tm", None, None, None),
        P("owner", "tm", None),
        P(),
        P(),
        P(),
    )
    return jax.shard_map(
        functools.partial(body, mesh.shape["tm"], mesh.shape["owner"]),
        mesh=mesh,
        in_specs=placed,
        out_specs=P("owner", "tm", None),
        check_vma=False,
    )
```

```python
import functools

import jax
import jax.numpy as jnp
from jax import lax
from jax.experimental import pallas as pl
from jax.experimental.pallas import tpu as pltpu
from jax.sharding import PartitionSpec as P

MESH = pl.DeviceIdType.MESH
PIECES = 4
LOCAL = 2
AHEAD = 2
LEND_AT = 0


def turn_kernel(n, w_ref, pat_ref, wt_ref, pg_ref, send_sem, recv_sem):
    m = lax.axis_index("tm")
    barrier = pltpu.get_barrier_semaphore()
    for step in range(1, n):
        pl.semaphore_signal(
            barrier, inc=1, device_id={"tm": lax.rem(m + step, n)}, device_id_type=MESH
        )
    pl.semaphore_wait(barrier, n - 1)

    def copy(step, landing):
        return pltpu.make_async_remote_copy(
            src_ref=pat_ref,
            dst_ref=pg_ref.at[landing],
            send_sem=send_sem.at[step],
            recv_sem=recv_sem.at[step],
            device_id={"tm": lax.rem(m + step, n)},
            device_id_type=MESH,
        )

    for step in range(1, n):
        copy(step, m).start()
    pg_ref[m] = pat_ref[...]
    rows = w_ref.shape[-1] // PIECES
    kp = w_ref.shape[1]

    def turn(i, carry):
        for k in range(kp):
            t = w_ref[i, k].T
            for c in range(PIECES):
                wt_ref[c, i, k] = t[c * rows : (c + 1) * rows]
        return carry

    lax.fori_loop(0, w_ref.shape[0], turn, 0)
    for step in range(1, n):
        copy(step, lax.rem(m - step + n, n)).wait_recv()
        copy(step, m).wait_send()


def turn(weights, pattern, n):
    fb, kp, faces, panels = weights.shape
    vmem = pl.BlockSpec(memory_space=pltpu.VMEM)
    return pl.pallas_call(
        functools.partial(turn_kernel, n),
        out_shape=(
            jax.ShapeDtypeStruct((PIECES, fb, kp, panels // PIECES, faces), weights.dtype),
            jax.ShapeDtypeStruct((n,) + pattern.shape, pattern.dtype),
        ),
        in_specs=[vmem] * 2,
        out_specs=(vmem, vmem),
        scratch_shapes=[
            pltpu.SemaphoreType.DMA((n,)),
            pltpu.SemaphoreType.DMA((n,)),
        ],
        compiler_params=pltpu.CompilerParams(
            collective_id=0, has_side_effects=True, vmem_limit_bytes=32 * 1024 * 1024
        ),
        name="turn_weights",
    )(weights, pattern)


def fused_kernel(
    n, owners, hit_ref, last_ref, w_ref, p_ref, out_ref,
    wg, terms, runs, outgoing, lent, outgoing2, wsend, wrecv, osend, orecv, own_sem, lent_sem, osend2,
):
    m = lax.axis_index("tm")
    me = lax.axis_index("owner")
    pieces, fb, kp, rows, block = w_ref.shape
    time_len = p_ref.shape[0]
    hits = terms.shape[0]
    slots = out_ref.shape[1]

    barrier = pltpu.get_barrier_semaphore()
    for step in range(1, n):
        pl.semaphore_signal(
            barrier, inc=1, device_id={"tm": lax.rem(m + step, n)}, device_id_type=MESH
        )
    for step in range(1, owners):
        pl.semaphore_signal(
            barrier, inc=1, device_id={"owner": lax.rem(me + step, owners)}, device_id_type=MESH
        )
    is_end = (m == 0) | (m == n - 1)
    helps = (m == 1) | (m == n - 2)
    near = jnp.where(m < n // 2, 1, n - 2)
    far = jnp.where(m < n // 2, 0, n - 1)

    @pl.when(is_end)
    def _():
        for step in range(owners):
            pl.semaphore_signal(
                barrier, inc=1, device_id={"tm": near, "owner": lax.rem(me + step, owners)},
                device_id_type=MESH,
            )

    pl.semaphore_wait(barrier, n + owners - 2 + jnp.where(helps, owners, 0))

    def lend():
        return pltpu.make_async_remote_copy(
            src_ref=p_ref,
            dst_ref=lent,
            send_sem=lent_sem.at[0],
            recv_sem=lent_sem.at[1],
            device_id={"tm": near},
            device_id_type=MESH,
        )

    def origin_of(way, hop):
        return jnp.clip(m - hop if way == 0 else m + hop, 0, n - 1)

    def send(way, hop, c):
        origin = origin_of(way, hop)
        toward = m + 1 if way == 0 else m - 1
        return pltpu.make_async_remote_copy(
            src_ref=w_ref.at[c] if hop == 0 else wg.at[c, origin],
            dst_ref=wg.at[c, origin],
            send_sem=wsend.at[way, hop, c],
            recv_sem=wrecv.at[way, hop, c],
            device_id={"tm": jnp.clip(toward, 0, n - 1)},
            device_id_type=MESH,
        )

    def landed(way, hop, c):
        return pltpu.make_async_remote_copy(
            src_ref=w_ref.at[c],
            dst_ref=wg.at[c, origin_of(way, hop + 1)],
            send_sem=wsend.at[way, hop, c],
            recv_sem=wrecv.at[way, hop, c],
            device_id={"tm": lax.rem(m + 1, n)},
            device_id_type=MESH,
        )

    def edge(c):
        return jnp.where(c >= LOCAL, 1, 0)

    def sends(way, hop, c):
        if way == 0:
            return (m - hop >= 0) & (m + 1 < n - edge(c))
        return (m + hop < n) & (m - 1 >= edge(c))

    def lands(way, hop, c):
        if way == 0:
            return (m - 1 - hop >= 0) & (m < n - edge(c))
        return (m + 1 + hop < n) & (m >= edge(c))

    def start_own(c):
        for way in range(2):
            @pl.when(sends(way, 0, c))
            def _():
                send(way, 0, c).start()

    def product(weights, origin, p_ref):
        for i in range(fb):
            face = origin * fb + i
            x = p_ref[:, pl.ds(pl.multiple_of(face * block, block), block)]
            y = lax.dot_general(
                weights(i).reshape(kp * rows, block), x, (((1,), (1,)), ((), ())),
                preferred_element_type=jnp.float32,
            )
            terms[pl.ds(face * kp, kp)] = y.reshape(kp, rows, time_len)

    def give(c, step, landing):
        peer = lax.rem(me + step, owners)
        return pltpu.make_async_remote_copy(
            src_ref=outgoing.at[c, peer],
            dst_ref=out_ref.at[landing, :, c],
            send_sem=osend.at[c, step],
            recv_sem=orecv.at[c, step],
            device_id={"owner": peer},
            device_id_type=MESH,
        )

    def keep(c):
        return pltpu.make_async_copy(outgoing.at[c, me], out_ref.at[me, :, c], own_sem.at[c])

    def give2(c, step, landing):
        peer = lax.rem(me + step, owners)
        return pltpu.make_async_remote_copy(
            src_ref=outgoing2.at[jnp.maximum(c - LOCAL, 0), peer],
            dst_ref=out_ref.at[landing, :, c],
            send_sem=osend2.at[c, step],
            recv_sem=orecv.at[c, step],
            device_id={"tm": far, "owner": peer},
            device_id_type=MESH,
        )

    def run(h, total):
        code = hit_ref[h]
        term = terms[code >> 1]
        total = jnp.where((code & 1) == 1, term, total + term)
        runs[h] = total
        return total

    def sum_up(target, at):
        lax.fori_loop(0, hits, run, jnp.zeros((rows, time_len), jnp.float32), unroll=8)
        for peer in range(owners):
            for slot in range(slots):
                code = last_ref[peer * slots + slot]
                total = runs[code >> 1]
                target[at, peer, slot] = jnp.where((code & 1) == 1, total, jnp.zeros_like(total))

    for c in range(AHEAD):
        start_own(c)

    def piece(c, carry):
        at_home = jnp.logical_not(is_end) | (c < LOCAL)

        @pl.when(at_home)
        def _():
            product(lambda i: w_ref[c, i], m, p_ref)

        for hop in range(n - 1):
            for way in range(2):
                @pl.when(lands(way, hop, c))
                def _():
                    landed(way, hop, c).wait_recv()
                if hop + 1 < n - 1:
                    @pl.when(sends(way, hop + 1, c))
                    def _():
                        send(way, hop + 1, c).start()
            if hop == 0:
                @pl.when(c + AHEAD < pieces)
                def _():
                    start_own(c + AHEAD)

                @pl.when(is_end & (c == LEND_AT))
                def _():
                    lend().start()

            for way in range(2):
                @pl.when(lands(way, hop, c))
                def _():
                    origin = origin_of(way, hop + 1)
                    product(lambda i: wg[c, origin, i], origin, p_ref)

        @pl.when(at_home)
        def _():
            sum_up(outgoing, c)
            for step in range(1, owners):
                give(c, step, me).start()
            keep(c).start()

        @pl.when(helps & (c == LOCAL))
        def _():
            lend().wait_recv()

        @pl.when(helps & (c >= LOCAL))
        def _():
            product(lambda i: w_ref[c, i], m, lent)

            def other(step, carry):
                origin = lax.rem(m + step, n)
                product(lambda i: wg[c, origin, i], origin, lent)
                return carry

            lax.fori_loop(1, n, other, 0)
            sum_up(outgoing2, c - LOCAL)
            for step in range(owners):
                give2(c, step, me).start()

        return carry

    lax.fori_loop(0, pieces, piece, 0)

    def finish(c, carry):
        at_home = jnp.logical_not(is_end) | (c < LOCAL)
        for hop in range(n - 1):
            for way in range(2):
                @pl.when(sends(way, hop, c))
                def _():
                    send(way, hop, c).wait_send()
        for step in range(1, owners):
            give(c, step, lax.rem(me - step + owners, owners)).wait_recv()

        @pl.when(at_home)
        def _():
            for step in range(1, owners):
                give(c, step, me).wait_send()
            keep(c).wait()

        @pl.when(jnp.logical_not(at_home))
        def _():
            give2(c, 0, me).wait_recv()

        @pl.when(helps & (c >= LOCAL))
        def _():
            for step in range(owners):
                give2(c, step, me).wait_send()

        return carry

    lax.fori_loop(0, pieces, finish, 0)

    @pl.when(is_end)
    def _():
        lend().wait_send()


def fused(hit, last, turned, pressure, n, owners):
    pieces, fb, kp, rows, block = turned.shape
    time_len = pressure.shape[0]
    slots = last.shape[0] // owners
    hits = hit.shape[0]
    smem = pl.BlockSpec(memory_space=pltpu.SMEM)
    vmem = pl.BlockSpec(memory_space=pltpu.VMEM)
    return pl.pallas_call(
        functools.partial(fused_kernel, n, owners),
        out_shape=jax.ShapeDtypeStruct((owners, slots, pieces, rows, time_len), jnp.float32),
        in_specs=[smem, smem, vmem, vmem],
        out_specs=pl.BlockSpec(memory_space=pl.ANY),
        scratch_shapes=[
            pltpu.VMEM((pieces, n, fb, kp, rows, block), turned.dtype),
            pltpu.VMEM((hits, rows, time_len), jnp.float32),
            pltpu.VMEM((hits, rows, time_len), jnp.float32),
            pltpu.VMEM((pieces, owners, slots, rows, time_len), jnp.float32),
            pltpu.VMEM(pressure.shape, pressure.dtype),
            pltpu.VMEM((pieces - LOCAL, owners, slots, rows, time_len), jnp.float32),
            pltpu.SemaphoreType.DMA((2, n - 1, pieces)),
            pltpu.SemaphoreType.DMA((2, n - 1, pieces)),
            pltpu.SemaphoreType.DMA((pieces, owners)),
            pltpu.SemaphoreType.DMA((pieces, owners)),
            pltpu.SemaphoreType.DMA((pieces,)),
            pltpu.SemaphoreType.DMA((2,)),
            pltpu.SemaphoreType.DMA((pieces, owners)),
        ],
        compiler_params=pltpu.CompilerParams(
            collective_id=1, has_side_effects=True, vmem_limit_bytes=48 * 1024 * 1024
        ),
        name="gather_multiply_exchange",
    )(hit, last, turned, pressure)


def hit_tables(rows, count):
    order = jnp.arange(rows.shape[0], dtype=jnp.int32)
    same = rows[:, None] == rows[None, :]
    before = order[None, :] < order[:, None]
    ahead = (rows[None, :] < rows[:, None]) | (same & before)
    rank = jnp.sum(ahead, axis=1, dtype=jnp.int32)
    first = 1 - jnp.any(same & before, axis=1).astype(jnp.int32)
    code = 2 * order + first
    hit = jnp.sum(
        jnp.where(rank[:, None] == order[None, :], code[:, None], 0), axis=0, dtype=jnp.int32
    )
    wanted = jnp.arange(count, dtype=jnp.int32)
    upto = jnp.sum(rows[None, :] <= wanted[:, None], axis=1, dtype=jnp.int32)
    there = jnp.any(rows[None, :] == wanted[:, None], axis=1).astype(jnp.int32)
    return hit, 2 * jnp.maximum(upto - 1, 0) + there


def collect_kernel(count, dest_ref, in_ref, out_ref):
    out_ref[...] = jnp.zeros_like(out_ref)

    def step(e, carry):
        out_ref[dest_ref[e]] += in_ref[e].T
        return carry

    lax.fori_loop(0, count, step, 0, unroll=4)


def collect(dest, received, capacity):
    count, block, time_len = received.shape
    return pl.pallas_call(
        functools.partial(collect_kernel, count),
        out_shape=jax.ShapeDtypeStruct((capacity, time_len, block), jnp.float32),
        grid_spec=pltpu.PrefetchScalarGridSpec(
            num_scalar_prefetch=1,
            grid=(1,),
            in_specs=[pl.BlockSpec(received.shape, lambda g, dest: (0, 0, 0))],
            out_specs=pl.BlockSpec(
                (capacity, time_len, block), lambda g, dest: (0, 0, 0)
            ),
        ),
        compiler_params=pltpu.CompilerParams(vmem_limit_bytes=32 * 1024 * 1024),
        name="collect",
    )(dest, received)


def tables(panel_list, owner_list, owner_count, own, slots):
    owners, list_len = panel_list.shape
    capacity = owner_list.shape[1]
    live = jnp.arange(capacity, dtype=jnp.int32)[None, :] < owner_count[:, None]
    listed = jnp.where(live, owner_list, -1).reshape(1, -1)
    place = jnp.arange(owners * capacity, dtype=jnp.int32)[None, :]
    found = jnp.sum(
        jnp.where(panel_list.reshape(-1, 1) == listed, place, 0), axis=1, dtype=jnp.int32
    ).reshape(owners, list_len)
    target, slot = found // capacity, found % capacity
    position = jnp.arange(list_len, dtype=jnp.int32)
    earlier = (target[:, None, :] == target[:, :, None]) & (
        position[None, None, :] < position[None, :, None]
    )
    rank = jnp.sum(earlier, axis=2, dtype=jnp.int32)
    packed_row = target * slots + rank
    wanted = own * slots + jnp.arange(slots, dtype=jnp.int32)
    dest = jnp.sum(
        jnp.where(packed_row[:, None, :] == wanted[None, :, None], slot[:, None, :], 0),
        axis=2,
        dtype=jnp.int32,
    )
    return packed_row[own], dest.reshape(-1)


def body(n_tm, n_owner, pressure, proj_weight, pattern, panel_list, owner_list, owner_count):
    own = lax.axis_index("owner")
    list_len = panel_list.shape[1]
    capacity = owner_list.shape[1]
    slots = list_len // n_owner
    packed_row, dest = tables(panel_list, owner_list, owner_count, own, slots)
    fb, kp = pattern.shape[1:]
    rows = packed_row[pattern[0].reshape(-1)].reshape(1, -1)
    rows = jnp.pad(rows, ((0, 7), (0, 128 - rows.shape[1])))
    turned, rows = turn(proj_weight[0], rows, n_tm)
    rows = rows[:, 0, : fb * kp].reshape(-1)
    hit, last = hit_tables(rows, list_len)
    received = fused(hit, last, turned, pressure, n_tm, n_owner)
    time_len = pressure.shape[0]
    return collect(dest, received.reshape(list_len, -1, time_len), capacity)


def solution(mesh):
    placed = (
        P("tm", "owner"),
        P("owner", "tm", None, None, None),
        P("owner", "tm", None),
        P(),
        P(),
        P(),
    )
    return jax.shard_map(
        functools.partial(body, mesh.shape["tm"], mesh.shape["owner"]),
        mesh=mesh,
        in_specs=placed,
        out_specs=P("owner", "tm", None),
        check_vma=False,
    )
```
